512 devices in a mesh: replica: 32 (over z, core), section: 16 (over y, x).
Axes of the slice: x: 4, y: 4, z: 16, core: 2. Of those that a mesh axis runs over, the one named last changes fastest.
Arguments:
- activations: bfloat16 [32, 16, 3, 128, 2688], P('replica', 'section'), may hold values from -64 to 64, as said below
- grad_output: bfloat16 [32, 128, 2688], P('replica'), may hold values from -6 to 6
- gains: float32 [16, 2688], replicated, may hold values from 0.1 to 1.9
- layer_section: int32 [32, 16], P('replica'), may hold values from 0 to 15, as said below
Outputs:
- gain_grad: float32 [16, 2688], P('section', 'replica')
- bias_grad: float32 [16, 2688], P('section', 'replica')
The draws below stay inside these ranges and needn't reach their ends.
Inputs may be any that keep to these rules, and one draw needn't show every extreme that they name: `layer_section`: each row does not decrease along the layers and starts at 0; its sections are consecutive, each from 0 to the row's largest holds 1 to 3 layers, and the row's largest is at least 9. Some section holds exactly 3 layers and some row uses all 16 sections. `activations`: entries of slots beyond a section's layers are not read.
All inputs are finite; a program needn't handle non-finite values.
Results may differ from the reference program's by a relative error of at most 0.011.
Values may be sent and summed in bfloat16 or wider, within the bound.
No kernel may reach another device: no remote copies, remote signals or barrier semaphores. Data moves between devices by JAX's collectives and lax.ppermute only.
A program may use at most 64 MiB of HBM per device.

```python
import math
import jax
import jax.numpy as jnp
from jax import lax

D = 2688
TOK = 128
MAXL = 3
SECTIONS = 16
REPLICAS = 32
LAYERS = 16


def shared_direction(key):
    key_dir, key_sign = jax.random.split(key)
    direction = jax.random.normal(key_dir, (REPLICAS, TOK, D), jnp.float32)
    signs = jnp.where(jax.random.bernoulli(key_sign, 0.5, (REPLICAS, TOK, 1)), 1.0, -1.0).astype(jnp.float32)
    return (direction, signs)


def draw_activations(key, part):
    direction, signs = shared_direction(key)
    key = jax.random.fold_in(key, 11)
    key_base, key_scale = jax.random.split(key, 2)
    shape = (REPLICAS, SECTIONS, MAXL, TOK, D)
    row_shape = (REPLICAS, SECTIONS, MAXL, TOK, 1)
    scales = jnp.exp(jax.random.uniform(key_scale, row_shape, jnp.float32, math.log(2.0), math.log(16.0)))
    aligned = 0.8 * direction[:, None, None, :, :]
    values = (jax.random.normal(key_base, shape, jnp.float32) + aligned) * scales
    return jnp.clip(values, -64.0, 64.0).astype(jnp.bfloat16)


def draw_grad_output(key, part):
    direction, signs = shared_direction(key)
    key = jax.random.fold_in(key, 17)
    shape = (REPLICAS, TOK, D)
    noise = jax.random.normal(key, shape, jnp.float32)
    values = 0.5 * signs * direction + noise
    return jnp.clip(values, -6.0, 6.0).astype(jnp.bfloat16)


def draw_layer_section(key, part):
    key = jax.random.fold_in(key, 23)
    key_count, key_heavy, key_order = jax.random.split(key, 3)
    lowest = 5 * SECTIONS // 8
    section_count = jax.random.randint(key_count, (REPLICAS,), lowest, SECTIONS + 1).astype(jnp.int32)
    section_count = section_count.at[0].set(lowest).at[1].set(SECTIONS)
    extra = LAYERS - section_count
    heavy = jax.random.randint(key_heavy, (REPLICAS,), 0, section_count).astype(jnp.int32)
    order = jax.vmap(lambda single: jax.random.permutation(single, SECTIONS))(jax.random.split(key_order, REPLICAS))
    section_ids = jnp.arange(SECTIONS).astype(jnp.int32)
    used = section_ids[None, :] < section_count[:, None]
    eligible = used & (section_ids[None, :] != heavy[:, None])
    earlier = order[:, None, :] < order[:, :, None]
    rank = jnp.sum((eligible[:, None, :] & earlier).astype(jnp.int32), axis=2)
    heavy_extra = jnp.minimum(extra, MAXL - 1)
    spread = eligible & (rank < (extra - heavy_extra)[:, None])
    per_section = used.astype(jnp.int32) + spread.astype(jnp.int32) + (section_ids[None, :] == heavy[:, None]).astype(jnp.int32) * heavy_extra[:, None]
    ends = jnp.cumsum(per_section, axis=1)
    layer_ids = jnp.arange(LAYERS).astype(jnp.int32)
    return jnp.sum((ends[:, None, :] <= layer_ids[None, :, None]).astype(jnp.int32), axis=2).astype(jnp.int32)


def setup_inputs(seed: int = 0) -> dict:
    key_list = jax.random.split(jax.random.key(seed), 5)
    return {
        "activations": draw_activations(jax.random.fold_in(key_list[4], 71), 0),
        "grad_output": draw_grad_output(jax.random.fold_in(key_list[4], 71), 0),
        "gains": jnp.clip(1.0 + 0.18 * jax.random.normal(key_list[2], (LAYERS, D), jnp.float32), 0.1, 1.9),
        "layer_section": draw_layer_section(jax.random.fold_in(key_list[4], 71), 0),
    }


epsilon = 1e-05

def reference(activations, grad_output, gains, layer_section):

    def one_replica(running, inputs):
        saved_inputs, start_grad, section_map = inputs
        below = lax.optimization_barrier(jnp.sum((section_map[None, :] < section_map[:, None]).astype(jnp.int32), axis=1))
        slot_ids = (jnp.arange(LAYERS).astype(jnp.int32) - below).astype(jnp.int32)

        def layer_step(gradient, layer_index):
            values = saved_inputs[section_map[layer_index], slot_ids[layer_index]].astype(jnp.float32)
            average = lax.optimization_barrier(jnp.mean(values, axis=-1, keepdims=True))
            centered = values - average
            variance = lax.optimization_barrier(jnp.mean(centered * centered, axis=-1, keepdims=True))
            inverse = lax.rsqrt(variance + epsilon)
            normed = centered * inverse
            incoming = gradient.astype(jnp.float32)
            scaled = gains[layer_index][None, :] * incoming
            update = scaled - lax.optimization_barrier(jnp.mean(scaled, axis=-1, keepdims=True)) - normed * lax.optimization_barrier(jnp.mean(scaled * normed, axis=-1, keepdims=True))
            outgoing = (incoming + inverse * update).astype(jnp.bfloat16)
            partial_value = jnp.stack([lax.optimization_barrier(jnp.sum(incoming * normed, axis=0)), lax.optimization_barrier(jnp.sum(incoming, axis=0))])
            return (outgoing, partial_value)
        order = jnp.arange(LAYERS - 1, -1, -1).astype(jnp.int32)
        final_grad, partials = lax.scan(layer_step, start_grad, order)
        return (running + partials, None)
    initial = jnp.zeros((LAYERS, 2, D), jnp.float32)
    summed, unused = lax.scan(one_replica, initial, (activations, grad_output, layer_section))
    summed = summed / REPLICAS
    return (summed[:, 0], summed[:, 1])
```

```python
import jax
import jax.numpy as jnp
from jax import lax
from jax.experimental import pallas as pl
from jax.experimental.pallas import tpu as pltpu
from jax.sharding import PartitionSpec as P

epsilon = 1e-05
lanes = 128


def total(terms):
    while len(terms) > 1:
        pairs = [left + right for left, right in zip(terms[::2], terms[1::2])]
        terms = pairs + terms[len(terms) - len(terms) % 2:]
    return terms[0]


def across(tile):
    return jnp.broadcast_to(jnp.sum(tile, axis=1, keepdims=True), tile.shape)


def fold(tiles):
    index = lax.broadcasted_iota(jnp.int32, tiles[0].shape, 0)
    low = index < 4
    quads = [
        jnp.where(low, a, b) + pltpu.roll(jnp.where(low, b, a), 4, 0) for a, b in zip(tiles[:4], tiles[4:])
    ]
    low = index % 4 < 2
    pairs = [
        jnp.where(low, a + pltpu.roll(a, 6, 0), b + pltpu.roll(b, 2, 0)) for a, b in zip(quads[:2], quads[2:])
    ]
    a, b = pairs
    return jnp.where(index % 2 < 1, a + pltpu.roll(a, 7, 0), b + pltpu.roll(b, 1, 0))


def relay_kernel(position_ref, map_ref, slots_ref, grad_ref, gains_ref, out_ref, held_ref, normed_ref, sem):
    layers, rows, channels = normed_ref.shape
    slot_count = slots_ref.shape[0] // out_ref.shape[0]
    columns = [slice(at, at + lanes) for at in range(0, channels, lanes)]
    share = 1.0 / channels
    fetch = pltpu.make_async_copy(grad_ref.at[position_ref[0]], held_ref, sem)
    fetch.start()
    places, slot = [], 0
    for layer in range(layers):
        if layer:
            slot = jnp.where(map_ref[layer] == map_ref[layer - 1], slot + 1, 0)
        places.append(map_ref[layer] * slot_count + slot)

    def tiles(layer):
        return [slots_ref[places[layer], :, at].astype(jnp.float32) for at in columns]

    order = list(reversed(range(layers)))
    average = {layer: across(total(tiles(layer))) * share for layer in order}
    inverse = {}
    for layer in order:
        centered = [tile - average[layer] for tile in tiles(layer)]
        inverse[layer] = lax.rsqrt(across(total([tile * tile for tile in centered])) * share + epsilon)
    for layer in order:
        for at, tile in zip(columns, tiles(layer)):
            normed_ref[layer, :, at] = (tile - average[layer]) * inverse[layer]
    fetch.wait()
    gradient = [held_ref[:, at].astype(jnp.float32) for at in columns]
    blank = jnp.zeros((rows, lanes), jnp.float32)
    for layer in order:
        normed = [normed_ref[layer, :, at] for at in columns]
        along = [g * n for g, n in zip(gradient, normed)]
        gain = [gains_ref[layer:layer + 1, at] for at in columns]
        scaled = [g * c for g, c in zip(gradient, gain)]
        along_one = across(total(scaled)) * share * inverse[layer]
        along_normed = across(total([p * c for p, c in zip(along, gain)])) * share * inverse[layer]
        sums = along + gradient
        sums = sums + [blank] * (-len(sums) % 16)
        row = layers - 1 - layer
        for at in range(0, len(sums), 16):
            packed = jnp.concatenate([fold(sums[at:at + 8]), fold(sums[at + 8:at + 16])], axis=0)
            out_ref[row, at:at + 16] = packed.astype(out_ref.dtype)
        gradient = [
            (g + inverse[layer] * u) - (along_one + along_normed * n)
            for g, u, n in zip(gradient, scaled, normed)
        ]


def relay(position, section_map, slots, grad, gains):
    layers, channels = gains.shape
    _, rows, _ = grad.shape
    packed_rows = -(-2 * channels // lanes // 16) * 16
    return pl.pallas_call(
        relay_kernel,
        grid_spec=pltpu.PrefetchScalarGridSpec(
            num_scalar_prefetch=2,
            grid=(),
            in_specs=[
                pl.BlockSpec(memory_space=pltpu.VMEM),
                pl.BlockSpec(memory_space=pl.ANY),
                pl.BlockSpec(memory_space=pltpu.VMEM),
            ],
            out_specs=pl.BlockSpec(memory_space=pltpu.VMEM),
            scratch_shapes=[
                pltpu.VMEM((rows, channels), grad.dtype),
                pltpu.VMEM((layers, rows, channels), jnp.float32),
                pltpu.SemaphoreType.DMA,
            ],
        ),
        out_shape=jax.ShapeDtypeStruct((layers, packed_rows, lanes), jnp.bfloat16),
        compiler_params=pltpu.CompilerParams(vmem_limit_bytes=24 * 1024 * 1024),
        cost_estimate=pl.CostEstimate(
            flops=30 * layers * rows * channels, bytes_accessed=4 * layers * rows * channels, transcendentals=0
        ),
    )(position, section_map, slots, grad, gains)


def summed(block, axis):
    received = lax.all_to_all(block, axis, 0, 0)
    return jnp.sum(received.astype(jnp.float32), axis=0)


def local(activations, grad_output, gains, layer_section):
    saved = activations[0, 0]
    slot_count, tokens, channels = saved.shape
    layers = gains.shape[0]
    sections = lax.axis_size("section")
    replicas = lax.axis_size("replica")
    position = jnp.full((1,), lax.axis_index("section"), jnp.int32)
    rows = tokens // sections
    blocks = saved.reshape(slot_count, sections, rows, channels)
    received = lax.all_to_all(blocks, "section", 1, 0)
    slots = received.reshape(sections * slot_count, rows, channels)
    grad = grad_output[0].reshape(sections, rows, channels)
    partials = relay(position, layer_section[0], slots, grad, gains)
    mine = summed(partials, "section")
    pieces = mine.reshape(-1)[: 2 * channels].reshape(2, replicas, channels // replicas)
    owned = summed(jnp.transpose(pieces, (1, 0, 2)), "replica") / replicas
    return (owned[:1], owned[1:])


def solution(mesh):
    placed = (
        P("replica", "section", None, None, None),
        P("replica", None, None),
        P(),
        P("replica", None),
    )
    return jax.shard_map(
        local,
        mesh=mesh,
        in_specs=placed,
        out_specs=(P("section", "replica"), P("section", "replica")),
        check_vma=False,
    )
```

```python
import jax
import jax.numpy as jnp
from jax import lax
from jax.experimental import pallas as pl
from jax.experimental.pallas import tpu as pltpu
from jax.sharding import PartitionSpec as P

epsilon = 1e-05
lanes = 128


def deal_kernel(saved_ref, out_ref, sems):
    slot_count, sections = saved_ref.shape[:2]
    parts = sems.shape[1]
    copies = []
    for slot in range(slot_count):
        for part in range(parts):
            at = pl.ds(part * (sections // parts), sections // parts)
            copies.append(pltpu.make_async_copy(saved_ref.at[slot, at], out_ref.at[at, slot], sems.at[slot, part]))
    for copy in copies:
        copy.start()
    for copy in copies:
        copy.wait()


def deal(saved):
    slot_count, sections, rows, channels = saved.shape
    return pl.pallas_call(
        deal_kernel,
        in_specs=[pl.BlockSpec(memory_space=pltpu.HBM)],
        out_specs=pl.BlockSpec(memory_space=pltpu.VMEM),
        scratch_shapes=[pltpu.SemaphoreType.DMA((slot_count, 4))],
        out_shape=jax.ShapeDtypeStruct((sections, slot_count, rows, channels), saved.dtype),
        compiler_params=pltpu.CompilerParams(vmem_limit_bytes=51 * 1024 * 1024),
        cost_estimate=pl.CostEstimate(flops=1, bytes_accessed=1, transcendentals=0),
    )(saved)


def total(terms):
    while len(terms) > 1:
        pairs = [left + right for left, right in zip(terms[::2], terms[1::2])]
        terms = pairs + terms[len(terms) - len(terms) % 2:]
    return terms[0]


def across(tile):
    return jnp.broadcast_to(jnp.sum(tile, axis=1, keepdims=True), tile.shape)


def fold(tiles):
    index = lax.broadcasted_iota(jnp.int32, tiles[0].shape, 0)
    low = index < 4
    quads = [
        jnp.where(low, a, b) + pltpu.roll(jnp.where(low, b, a), 4, 0) for a, b in zip(tiles[:4], tiles[4:])
    ]
    low = index % 4 < 2
    pairs = [
        jnp.where(low, a + pltpu.roll(a, 6, 0), b + pltpu.roll(b, 2, 0)) for a, b in zip(quads[:2], quads[2:])
    ]
    a, b = pairs
    return jnp.where(index % 2 < 1, a + pltpu.roll(a, 7, 0), b + pltpu.roll(b, 1, 0))


def relay_kernel(position_ref, map_ref, slots_ref, grad_ref, gains_ref, out_ref, held_ref, normed_ref, sem):
    layers, rows, channels = normed_ref.shape
    slot_count = slots_ref.shape[0] // out_ref.shape[0]
    columns = [slice(at, at + lanes) for at in range(0, channels, lanes)]
    share = 1.0 / channels
    fetch = pltpu.make_async_copy(grad_ref.at[position_ref[0]], held_ref, sem)
    fetch.start()
    places, slot = [], 0
    for layer in range(layers):
        if layer:
            slot = jnp.where(map_ref[layer] == map_ref[layer - 1], slot + 1, 0)
        places.append(map_ref[layer] * slot_count + slot)

    def tiles(layer):
        return [slots_ref[places[layer], :, at].astype(jnp.float32) for at in columns]

    order = list(reversed(range(layers)))
    average = {layer: across(total(tiles(layer))) * share for layer in order}
    inverse = {}
    for layer in order:
        centered = [tile - average[layer] for tile in tiles(layer)]
        inverse[layer] = lax.rsqrt(across(total([tile * tile for tile in centered])) * share + epsilon)
    for layer in order:
        for at, tile in zip(columns, tiles(layer)):
            normed_ref[layer, :, at] = (tile - average[layer]) * inverse[layer]
    fetch.wait()
    gradient = [held_ref[:, at].astype(jnp.float32) for at in columns]
    blank = jnp.zeros((rows, lanes), jnp.float32)
    for layer in order:
        normed = [normed_ref[layer, :, at] for at in columns]
        along = [g * n for g, n in zip(gradient, normed)]
        gain = [gains_ref[layer:layer + 1, at] for at in columns]
        scaled = [g * c for g, c in zip(gradient, gain)]
        along_one = across(total(scaled)) * share * inverse[layer]
        along_normed = across(total([p * c for p, c in zip(along, gain)])) * share * inverse[layer]
        sums = along + gradient
        sums = sums + [blank] * (-len(sums) % 16)
        row = layers - 1 - layer
        for at in range(0, len(sums), 16):
            packed = jnp.concatenate([fold(sums[at:at + 8]), fold(sums[at + 8:at + 16])], axis=0)
            out_ref[row, at:at + 16] = packed.astype(out_ref.dtype)
        gradient = [
            (g + inverse[layer] * u) - (along_one + along_normed * n)
            for g, u, n in zip(gradient, scaled, normed)
        ]


def relay(position, section_map, slots, grad, gains):
    layers, channels = gains.shape
    _, rows, _ = grad.shape
    packed_rows = -(-2 * channels // lanes // 16) * 16
    return pl.pallas_call(
        relay_kernel,
        grid_spec=pltpu.PrefetchScalarGridSpec(
            num_scalar_prefetch=2,
            grid=(),
            in_specs=[
                pl.BlockSpec(memory_space=pltpu.VMEM),
                pl.BlockSpec(memory_space=pl.ANY),
                pl.BlockSpec(memory_space=pltpu.VMEM),
            ],
            out_specs=pl.BlockSpec(memory_space=pltpu.VMEM),
            scratch_shapes=[
                pltpu.VMEM((rows, channels), grad.dtype),
                pltpu.VMEM((layers, rows, channels), jnp.float32),
                pltpu.SemaphoreType.DMA,
            ],
        ),
        out_shape=jax.ShapeDtypeStruct((layers, packed_rows, lanes), jnp.bfloat16),
        compiler_params=pltpu.CompilerParams(vmem_limit_bytes=24 * 1024 * 1024),
        cost_estimate=pl.CostEstimate(
            flops=30 * layers * rows * channels, bytes_accessed=4 * layers * rows * channels, transcendentals=0
        ),
    )(position, section_map, slots, grad, gains)


def summed(block, axis):
    received = lax.all_to_all(block, axis, 0, 0)
    return jnp.sum(received.astype(jnp.float32), axis=0)


def local(activations, grad_output, gains, layer_section):
    saved = activations[0, 0]
    slot_count, tokens, channels = saved.shape
    layers = gains.shape[0]
    sections = lax.axis_size("section")
    replicas = lax.axis_size("replica")
    position = jnp.full((1,), lax.axis_index("section"), jnp.int32)
    rows = tokens // sections
    blocks = deal(saved.reshape(slot_count, sections, rows, channels))
    received = lax.all_to_all(blocks, "section", 0, 0)
    slots = received.reshape(sections * slot_count, rows, channels)
    grad = grad_output[0].reshape(sections, rows, channels)
    partials = relay(position, layer_section[0], slots, grad, gains)
    mine = summed(partials, "section")
    pieces = mine.reshape(-1)[: 2 * channels].reshape(2, replicas, channels // replicas)
    owned = summed(jnp.transpose(pieces, (1, 0, 2)), "replica") / replicas
    return (owned[:1], owned[1:])


def solution(mesh):
    placed = (
        P("replica", "section", None, None, None),
        P("replica", None, None),
        P(),
        P("replica", None),
    )
    return jax.shard_map(
        local,
        mesh=mesh,
        in_specs=placed,
        out_specs=(P("section", "replica"), P("section", "replica")),
        check_vma=False,
    )
```

```python
import jax
import jax.numpy as jnp
from jax import lax
from jax.experimental import pallas as pl
from jax.experimental.pallas import tpu as pltpu
from jax.sharding import PartitionSpec as P

epsilon = 1e-05
lanes = 128


def deal_kernel(saved_ref, out_ref, held_ref, in_sems, out_sems):
    slot_count, sections = saved_ref.shape[:2]
    parts = in_sems.shape[1]
    step = sections // parts
    inward, outward = [], []
    for part in range(parts):
        for slot in range(slot_count):
            at = pl.ds(part * step, step)
            held = held_ref.at[slot, at]
            inward.append(pltpu.make_async_copy(saved_ref.at[slot, at], held, in_sems.at[slot, part]))
            outward.append(pltpu.make_async_copy(held, out_ref.at[at, slot], out_sems.at[slot, part]))
    for copy in inward:
        copy.start()
    for copy, onward in zip(inward, outward):
        copy.wait()
        onward.start()
    for onward in outward:
        onward.wait()


def deal(saved):
    slot_count, sections, rows, channels = saved.shape
    return pl.pallas_call(
        deal_kernel,
        in_specs=[pl.BlockSpec(memory_space=pltpu.HBM)],
        out_specs=pl.BlockSpec(memory_space=pltpu.HBM),
        scratch_shapes=[
            pltpu.VMEM(saved.shape, saved.dtype),
            pltpu.SemaphoreType.DMA((slot_count, 8)),
            pltpu.SemaphoreType.DMA((slot_count, 8)),
        ],
        out_shape=jax.ShapeDtypeStruct((sections, slot_count, rows, channels), saved.dtype),
        compiler_params=pltpu.CompilerParams(vmem_limit_bytes=56 * 1024 * 1024),
        cost_estimate=pl.CostEstimate(flops=1, bytes_accessed=1, transcendentals=0),
    )(saved)


def total(terms):
    while len(terms) > 1:
        pairs = [left + right for left, right in zip(terms[::2], terms[1::2])]
        terms = pairs + terms[len(terms) - len(terms) % 2:]
    return terms[0]


def across(tile):
    return jnp.broadcast_to(jnp.sum(tile, axis=1, keepdims=True), tile.shape)


def fold(tiles):
    index = lax.broadcasted_iota(jnp.int32, tiles[0].shape, 0)
    low = index < 4
    quads = [
        jnp.where(low, a, b) + pltpu.roll(jnp.where(low, b, a), 4, 0) for a, b in zip(tiles[:4], tiles[4:])
    ]
    low = index % 4 < 2
    pairs = [
        jnp.where(low, a + pltpu.roll(a, 6, 0), b + pltpu.roll(b, 2, 0)) for a, b in zip(quads[:2], quads[2:])
    ]
    a, b = pairs
    return jnp.where(index % 2 < 1, a + pltpu.roll(a, 7, 0), b + pltpu.roll(b, 1, 0))


def relay_kernel(position_ref, map_ref, slots_ref, grad_ref, gains_ref, out_ref, held_ref, normed_ref, sem):
    layers, rows, channels = normed_ref.shape
    slot_count = slots_ref.shape[0] // out_ref.shape[0]
    columns = [slice(at, at + lanes) for at in range(0, channels, lanes)]
    share = 1.0 / channels
    fetch = pltpu.make_async_copy(grad_ref.at[position_ref[0]], held_ref, sem)
    fetch.start()
    places, slot = [], 0
    for layer in range(layers):
        if layer:
            slot = jnp.where(map_ref[layer] == map_ref[layer - 1], slot + 1, 0)
        places.append(map_ref[layer] * slot_count + slot)

    def tiles(layer):
        return [slots_ref[places[layer], :, at].astype(jnp.float32) for at in columns]

    order = list(reversed(range(layers)))
    average = {layer: across(total(tiles(layer))) * share for layer in order}
    inverse = {}
    for layer in order:
        centered = [tile - average[layer] for tile in tiles(layer)]
        inverse[layer] = lax.rsqrt(across(total([tile * tile for tile in centered])) * share + epsilon)
    for layer in order:
        for at, tile in zip(columns, tiles(layer)):
            normed_ref[layer, :, at] = (tile - average[layer]) * inverse[layer]
    fetch.wait()
    gradient = [held_ref[:, at].astype(jnp.float32) for at in columns]
    blank = jnp.zeros((rows, lanes), jnp.float32)
    for layer in order:
        normed = [normed_ref[layer, :, at] for at in columns]
        along = [g * n for g, n in zip(gradient, normed)]
        gain = [gains_ref[layer:layer + 1, at] for at in columns]
        scaled = [g * c for g, c in zip(gradient, gain)]
        along_one = across(total(scaled)) * share * inverse[layer]
        along_normed = across(total([p * c for p, c in zip(along, gain)])) * share * inverse[layer]
        sums = along + gradient
        sums = sums + [blank] * (-len(sums) % 16)
        row = layers - 1 - layer
        for at in range(0, len(sums), 16):
            packed = jnp.concatenate([fold(sums[at:at + 8]), fold(sums[at + 8:at + 16])], axis=0)
            out_ref[row, at:at + 16] = packed.astype(out_ref.dtype)
        gradient = [
            (g + inverse[layer] * u) - (along_one + along_normed * n)
            for g, u, n in zip(gradient, scaled, normed)
        ]


def relay(position, section_map, slots, grad, gains):
    layers, channels = gains.shape
    _, rows, _ = grad.shape
    packed_rows = -(-2 * channels // lanes // 16) * 16
    return pl.pallas_call(
        relay_kernel,
        grid_spec=pltpu.PrefetchScalarGridSpec(
            num_scalar_prefetch=2,
            grid=(),
            in_specs=[
                pl.BlockSpec(memory_space=pltpu.VMEM),
                pl.BlockSpec(memory_space=pl.ANY),
                pl.BlockSpec(memory_space=pltpu.VMEM),
            ],
            out_specs=pl.BlockSpec(memory_space=pltpu.VMEM),
            scratch_shapes=[
                pltpu.VMEM((rows, channels), grad.dtype),
                pltpu.VMEM((layers, rows, channels), jnp.float32),
                pltpu.SemaphoreType.DMA,
            ],
        ),
        out_shape=jax.ShapeDtypeStruct((layers, packed_rows, lanes), jnp.bfloat16),
        compiler_params=pltpu.CompilerParams(vmem_limit_bytes=24 * 1024 * 1024),
        cost_estimate=pl.CostEstimate(
            flops=30 * layers * rows * channels, bytes_accessed=4 * layers * rows * channels, transcendentals=0
        ),
    )(position, section_map, slots, grad, gains)


def summed(block, axis):
    received = lax.all_to_all(block, axis, 0, 0)
    return jnp.sum(received.astype(jnp.float32), axis=0)


def local(activations, grad_output, gains, layer_section):
    saved = activations[0, 0]
    slot_count, tokens, channels = saved.shape
    layers = gains.shape[0]
    sections = lax.axis_size("section")
    replicas = lax.axis_size("replica")
    position = jnp.full((1,), lax.axis_index("section"), jnp.int32)
    rows = tokens // sections
    blocks = deal(saved.reshape(slot_count, sections, rows, channels))
    received = lax.all_to_all(blocks, "section", 0, 0)
    slots = received.reshape(sections * slot_count, rows, channels)
    grad = grad_output[0].reshape(sections, rows, channels)
    partials = relay(position, layer_section[0], slots, grad, gains)
    mine = summed(partials, "section")
    pieces = mine.reshape(-1)[: 2 * channels].reshape(2, replicas, channels // replicas)
    owned = summed(jnp.transpose(pieces, (1, 0, 2)), "replica") / replicas
    return (owned[:1], owned[1:])


def solution(mesh):
    placed = (
        P("replica", "section", None, None, None),
        P("replica", None, None),
        P(),
        P("replica", None),
    )
    return jax.shard_map(
        local,
        mesh=mesh,
        in_specs=placed,
        out_specs=(P("section", "replica"), P("section", "replica")),
        check_vma=False,
    )
```

```python
import jax
import jax.numpy as jnp
from jax import lax
from jax.experimental import pallas as pl
from jax.experimental.pallas import tpu as pltpu
from jax.sharding import PartitionSpec as P

epsilon = 1e-05
lanes = 128


def deal_kernel(saved_ref, out_ref, held_ref, in_sems, out_sems):
    slot_count, sections = saved_ref.shape[:2]
    parts = in_sems.shape[1]
    step = sections // parts
    inward, outward = [], []
    for part in range(parts):
        for slot in range(slot_count):
            at = pl.ds(part * step, step)
            held = held_ref.at[slot, at]
            inward.append(pltpu.make_async_copy(saved_ref.at[slot, at], held, in_sems.at[slot, part]))
            outward.append(pltpu.make_async_copy(held, out_ref.at[at, slot], out_sems.at[slot, part]))
    for copy in inward:
        copy.start()
    for copy, onward in zip(inward, outward):
        copy.wait()
        onward.start()
    for onward in outward:
        onward.wait()


def deal(saved):
    slot_count, sections, rows, channels = saved.shape
    return pl.pallas_call(
        deal_kernel,
        in_specs=[pl.BlockSpec(memory_space=pltpu.HBM)],
        out_specs=pl.BlockSpec(memory_space=pltpu.HBM),
        scratch_shapes=[
            pltpu.VMEM(saved.shape, saved.dtype),
            pltpu.SemaphoreType.DMA((slot_count, 8)),
            pltpu.SemaphoreType.DMA((slot_count, 8)),
        ],
        out_shape=jax.ShapeDtypeStruct((sections, slot_count, rows, channels), saved.dtype),
        compiler_params=pltpu.CompilerParams(vmem_limit_bytes=56 * 1024 * 1024),
        cost_estimate=pl.CostEstimate(flops=1, bytes_accessed=1, transcendentals=0),
    )(saved)


def total(terms):
    while len(terms) > 1:
        pairs = [left + right for left, right in zip(terms[::2], terms[1::2])]
        terms = pairs + terms[len(terms) - len(terms) % 2:]
    return terms[0]


def across(tile):
    return jnp.broadcast_to(jnp.sum(tile, axis=1, keepdims=True), tile.shape)


def fold(tiles):
    index = lax.broadcasted_iota(jnp.int32, tiles[0].shape, 0)
    low = index < 4
    quads = [
        jnp.where(low, a, b) + pltpu.roll(jnp.where(low, b, a), 4, 0) for a, b in zip(tiles[:4], tiles[4:])
    ]
    low = index % 4 < 2
    pairs = [
        jnp.where(low, a + pltpu.roll(a, 6, 0), b + pltpu.roll(b, 2, 0)) for a, b in zip(quads[:2], quads[2:])
    ]
    a, b = pairs
    return jnp.where(index % 2 < 1, a + pltpu.roll(a, 7, 0), b + pltpu.roll(b, 1, 0))


def relay_kernel(position_ref, map_ref, slots_ref, grad_ref, gains_ref, out_ref, held_ref, normed_ref, sem):
    layers, rows, channels = normed_ref.shape
    slot_count = slots_ref.shape[0] // out_ref.shape[0]
    columns = [slice(at, at + lanes) for at in range(0, channels, lanes)]
    share = 1.0 / channels
    fetch = pltpu.make_async_copy(grad_ref.at[position_ref[0]], held_ref, sem)
    fetch.start()
    places, slot = [], 0
    for layer in range(layers):
        if layer:
            slot = jnp.where(map_ref[layer] == map_ref[layer - 1], slot + 1, 0)
        places.append(map_ref[layer] * slot_count + slot)

    def tiles(layer):
        return [slots_ref[places[layer], :, at].astype(jnp.float32) for at in columns]

    order = list(reversed(range(layers)))
    average = {layer: across(total(tiles(layer))) * share for layer in order}
    inverse = {}
    for layer in order:
        centered = [tile - average[layer] for tile in tiles(layer)]
        inverse[layer] = lax.rsqrt(across(total([tile * tile for tile in centered])) * share + epsilon)
    for layer in order:
        for at, tile in zip(columns, tiles(layer)):
            normed_ref[layer, :, at] = (tile - average[layer]) * inverse[layer]
    fetch.wait()
    gradient = [held_ref[:, at].astype(jnp.float32) for at in columns]
    blank = jnp.zeros((rows, lanes), jnp.float32)
    for layer in order:
        normed = [normed_ref[layer, :, at] for at in columns]
        along = [g * n for g, n in zip(gradient, normed)]
        gain = [gains_ref[layer:layer + 1, at] for at in columns]
        scaled = [g * c for g, c in zip(gradient, gain)]
        along_one = across(total(scaled)) * share * inverse[layer]
        along_normed = across(total([p * c for p, c in zip(along, gain)])) * share * inverse[layer]
        sums = along + gradient
        sums = sums + [blank] * (-len(sums) % 16)
        row = layers - 1 - layer
        for at in range(0, len(sums), 16):
            packed = jnp.concatenate([fold(sums[at:at + 8]), fold(sums[at + 8:at + 16])], axis=0)
            out_ref[row, at:at + 16] = packed.astype(out_ref.dtype)
        gradient = [
            ((g + inverse[layer] * u) - (along_one + along_normed * n)).astype(jnp.bfloat16).astype(jnp.float32)
            for g, u, n in zip(gradient, scaled, normed)
        ]


def relay(position, section_map, slots, grad, gains):
    layers, channels = gains.shape
    _, rows, _ = grad.shape
    packed_rows = -(-2 * channels // lanes // 16) * 16
    return pl.pallas_call(
        relay_kernel,
        grid_spec=pltpu.PrefetchScalarGridSpec(
            num_scalar_prefetch=2,
            grid=(),
            in_specs=[
                pl.BlockSpec(memory_space=pltpu.VMEM),
                pl.BlockSpec(memory_space=pl.ANY),
                pl.BlockSpec(memory_space=pltpu.VMEM),
            ],
            out_specs=pl.BlockSpec(memory_space=pltpu.VMEM),
            scratch_shapes=[
                pltpu.VMEM((rows, channels), grad.dtype),
                pltpu.VMEM((layers, rows, channels), jnp.float32),
                pltpu.SemaphoreType.DMA,
            ],
        ),
        out_shape=jax.ShapeDtypeStruct((layers, packed_rows, lanes), jnp.bfloat16),
        compiler_params=pltpu.CompilerParams(vmem_limit_bytes=24 * 1024 * 1024),
        cost_estimate=pl.CostEstimate(
            flops=30 * layers * rows * channels, bytes_accessed=4 * layers * rows * channels, transcendentals=0
        ),
    )(position, section_map, slots, grad, gains)


def summed(block, axis):
    received = lax.all_to_all(block, axis, 0, 0)
    return jnp.sum(received.astype(jnp.float32), axis=0)


def local(activations, grad_output, gains, layer_section):
    saved = activations[0, 0]
    slot_count, tokens, channels = saved.shape
    layers = gains.shape[0]
    sections = lax.axis_size("section")
    replicas = lax.axis_size("replica")
    position = jnp.full((1,), lax.axis_index("section"), jnp.int32)
    rows = tokens // sections
    blocks = deal(saved.reshape(slot_count, sections, rows, channels))
    received = lax.all_to_all(blocks, "section", 0, 0)
    slots = received.reshape(sections * slot_count, rows, channels)
    grad = grad_output[0].reshape(sections, rows, channels)
    partials = relay(position, layer_section[0], slots, grad, gains)
    mine = summed(partials, "section")
    pieces = mine.reshape(-1)[: 2 * channels].reshape(2, replicas, channels // replicas)
    owned = summed(jnp.transpose(pieces, (1, 0, 2)), "replica") / replicas
    return (owned[:1], owned[1:])


def solution(mesh):
    placed = (
        P("replica", "section", None, None, None),
        P("replica", None, None),
        P(),
        P("replica", None),
    )
    return jax.shard_map(
        local,
        mesh=mesh,
        in_specs=placed,
        out_specs=(P("section", "replica"), P("section", "replica")),
        check_vma=False,
    )
```

```python
import jax
import jax.numpy as jnp
from jax import lax
from jax.experimental import pallas as pl
from jax.experimental.pallas import tpu as pltpu
from jax.sharding import PartitionSpec as P

epsilon = 1e-05
lanes = 128


def deal_kernel(saved_ref, out_ref, held_ref, in_sems, out_sems):
    slot_count, sections = saved_ref.shape[:2]
    parts = in_sems.shape[1]
    step = sections // parts
    inward, outward = [], []
    for part in range(parts):
        for slot in range(slot_count):
            at = pl.ds(part * step, step)
            held = held_ref.at[slot, at]
            inward.append(pltpu.make_async_copy(saved_ref.at[slot, at], held, in_sems.at[slot, part]))
            outward.append(pltpu.make_async_copy(held, out_ref.at[at, slot], out_sems.at[slot, part]))
    ahead = 6
    for copy in inward[:ahead]:
        copy.start()
    for index, (copy, onward) in enumerate(zip(inward, outward)):
        copy.wait()
        onward.start()
        if index + ahead < len(inward):
            inward[index + ahead].start()
    for onward in outward:
        onward.wait()


def deal(saved):
    slot_count, sections, rows, channels = saved.shape
    return pl.pallas_call(
        deal_kernel,
        in_specs=[pl.BlockSpec(memory_space=pltpu.HBM)],
        out_specs=pl.BlockSpec(memory_space=pltpu.HBM),
        scratch_shapes=[
            pltpu.VMEM(saved.shape, saved.dtype),
            pltpu.SemaphoreType.DMA((slot_count, 8)),
            pltpu.SemaphoreType.DMA((slot_count, 8)),
        ],
        out_shape=jax.ShapeDtypeStruct((sections, slot_count, rows, channels), saved.dtype),
        compiler_params=pltpu.CompilerParams(vmem_limit_bytes=56 * 1024 * 1024),
        cost_estimate=pl.CostEstimate(flops=1, bytes_accessed=1, transcendentals=0),
    )(saved)


def total(terms):
    while len(terms) > 1:
        pairs = [left + right for left, right in zip(terms[::2], terms[1::2])]
        terms = pairs + terms[len(terms) - len(terms) % 2:]
    return terms[0]


def across(tile):
    return jnp.broadcast_to(jnp.sum(tile, axis=1, keepdims=True), tile.shape)


def fold(tiles):
    index = lax.broadcasted_iota(jnp.int32, tiles[0].shape, 0)
    low = index < 4
    quads = [
        jnp.where(low, a, b) + pltpu.roll(jnp.where(low, b, a), 4, 0) for a, b in zip(tiles[:4], tiles[4:])
    ]
    low = index % 4 < 2
    pairs = [
        jnp.where(low, a + pltpu.roll(a, 6, 0), b + pltpu.roll(b, 2, 0)) for a, b in zip(quads[:2], quads[2:])
    ]
    a, b = pairs
    return jnp.where(index % 2 < 1, a + pltpu.roll(a, 7, 0), b + pltpu.roll(b, 1, 0))


def relay_kernel(position_ref, map_ref, slots_ref, grad_ref, gains_ref, out_ref, held_ref, centered_ref, sem):
    layers, rows, channels = centered_ref.shape
    slot_count = slots_ref.shape[0] // out_ref.shape[0]
    columns = [slice(at, at + lanes) for at in range(0, channels, lanes)]
    share = 1.0 / channels
    fetch = pltpu.make_async_copy(grad_ref.at[position_ref[0]], held_ref, sem)
    fetch.start()
    places, slot = [], 0
    for layer in range(layers):
        if layer:
            slot = jnp.where(map_ref[layer] == map_ref[layer - 1], slot + 1, 0)
        places.append(map_ref[layer] * slot_count + slot)

    def tiles(layer):
        return [slots_ref[places[layer], :, at].astype(jnp.float32) for at in columns]

    order = list(reversed(range(layers)))
    average = {layer: across(total(tiles(layer))) * share for layer in order}
    inverse = {}
    for layer in order:
        centered = [tile - average[layer] for tile in tiles(layer)]
        for at, tile in zip(columns, centered):
            centered_ref[layer, :, at] = tile
        inverse[layer] = lax.rsqrt(across(total([tile * tile for tile in centered])) * share + epsilon)
    fetch.wait()
    gradient = [held_ref[:, at].astype(jnp.float32) for at in columns]
    blank = jnp.zeros((rows, lanes), jnp.float32)
    for layer in order:
        normed = [centered_ref[layer, :, at] * inverse[layer] for at in columns]
        weight = inverse[layer] * share
        along = [g * n for g, n in zip(gradient, normed)]
        gain = [gains_ref[layer:layer + 1, at] for at in columns]
        scaled = [g * c for g, c in zip(gradient, gain)]
        along_one = across(total(scaled)) * weight
        along_normed = across(total([p * c for p, c in zip(along, gain)])) * weight
        sums = along + gradient
        sums = sums + [blank] * (-len(sums) % 16)
        row = layers - 1 - layer
        for at in range(0, len(sums), 16):
            packed = jnp.concatenate([fold(sums[at:at + 8]), fold(sums[at + 8:at + 16])], axis=0)
            out_ref[row, at:at + 16] = packed.astype(out_ref.dtype)
        gradient = [
            ((g + inverse[layer] * u) - (along_one + along_normed * n)).astype(jnp.bfloat16).astype(jnp.float32)
            for g, u, n in zip(gradient, scaled, normed)
        ]


def relay(position, section_map, slots, grad, gains):
    layers, channels = gains.shape
    _, rows, _ = grad.shape
    packed_rows = -(-2 * channels // lanes // 16) * 16
    return pl.pallas_call(
        relay_kernel,
        grid_spec=pltpu.PrefetchScalarGridSpec(
            num_scalar_prefetch=2,
            grid=(),
            in_specs=[
                pl.BlockSpec(memory_space=pltpu.VMEM),
                pl.BlockSpec(memory_space=pl.ANY),
                pl.BlockSpec(memory_space=pltpu.VMEM),
            ],
            out_specs=pl.BlockSpec(memory_space=pltpu.VMEM),
            scratch_shapes=[
                pltpu.VMEM((rows, channels), grad.dtype),
                pltpu.VMEM((layers, rows, channels), jnp.float32),
                pltpu.SemaphoreType.DMA,
            ],
        ),
        out_shape=jax.ShapeDtypeStruct((layers, packed_rows, lanes), jnp.bfloat16),
        compiler_params=pltpu.CompilerParams(vmem_limit_bytes=24 * 1024 * 1024),
        cost_estimate=pl.CostEstimate(
            flops=30 * layers * rows * channels, bytes_accessed=4 * layers * rows * channels, transcendentals=0
        ),
    )(position, section_map, slots, grad, gains)


def summed(block, axis):
    received = lax.all_to_all(block, axis, 0, 0)
    return jnp.sum(received.astype(jnp.float32), axis=0)


def local(activations, grad_output, gains, layer_section):
    saved = activations[0, 0]
    slot_count, tokens, channels = saved.shape
    layers = gains.shape[0]
    sections = lax.axis_size("section")
    replicas = lax.axis_size("replica")
    position = jnp.full((1,), lax.axis_index("section"), jnp.int32)
    rows = tokens // sections
    blocks = deal(saved.reshape(slot_count, sections, rows, channels))
    received = lax.all_to_all(blocks, "section", 0, 0)
    slots = received.reshape(sections * slot_count, rows, channels)
    grad = grad_output[0].reshape(sections, rows, channels)
    partials = relay(position, layer_section[0], slots, grad, gains)
    mine = summed(partials, "section")
    pieces = mine.reshape(-1)[: 2 * channels].reshape(2, replicas, channels // replicas)
    owned = summed(jnp.transpose(pieces, (1, 0, 2)), "replica") / replicas
    return (owned[:1], owned[1:])


def solution(mesh):
    placed = (
        P("replica", "section", None, None, None),
        P("replica", None, None),
        P(),
        P("replica", None),
    )
    return jax.shard_map(
        local,
        mesh=mesh,
        in_specs=placed,
        out_specs=(P("section", "replica"), P("section", "replica")),
        check_vma=False,
    )
```

```python
import jax
import jax.numpy as jnp
from jax import lax
from jax.experimental import pallas as pl
from jax.experimental.pallas import tpu as pltpu
from jax.sharding import PartitionSpec as P

epsilon = 1e-05
lanes = 128


def deal_kernel(saved_ref, out_ref, held_ref, in_sems, out_sems):
    slot_count, sections = saved_ref.shape[:2]
    parts = in_sems.shape[1]
    step = sections // parts
    inward, outward = [], []
    for part in range(parts):
        for slot in range(slot_count):
            at = pl.ds(part * step, step)
            held = held_ref.at[slot, at]
            inward.append(pltpu.make_async_copy(saved_ref.at[slot, at], held, in_sems.at[slot, part]))
            outward.append(pltpu.make_async_copy(held, out_ref.at[at, slot], out_sems.at[slot, part]))
    for copy in inward:
        copy.start()
    for copy, onward in zip(inward, outward):
        copy.wait()
        onward.start(priority=1)
    for onward in outward:
        onward.wait()


def deal(saved):
    slot_count, sections, rows, channels = saved.shape
    return pl.pallas_call(
        deal_kernel,
        in_specs=[pl.BlockSpec(memory_space=pltpu.HBM)],
        out_specs=pl.BlockSpec(memory_space=pltpu.HBM),
        scratch_shapes=[
            pltpu.VMEM(saved.shape, saved.dtype),
            pltpu.SemaphoreType.DMA((slot_count, 8)),
            pltpu.SemaphoreType.DMA((slot_count, 8)),
        ],
        out_shape=jax.ShapeDtypeStruct((sections, slot_count, rows, channels), saved.dtype),
        compiler_params=pltpu.CompilerParams(vmem_limit_bytes=56 * 1024 * 1024),
        cost_estimate=pl.CostEstimate(flops=1, bytes_accessed=1, transcendentals=0),
    )(saved)


def total(terms):
    while len(terms) > 1:
        pairs = [left + right for left, right in zip(terms[::2], terms[1::2])]
        terms = pairs + terms[len(terms) - len(terms) % 2:]
    return terms[0]


def across(tile):
    return jnp.broadcast_to(jnp.sum(tile, axis=1, keepdims=True), tile.shape)


def fold(tiles):
    index = lax.broadcasted_iota(jnp.int32, tiles[0].shape, 0)
    low = index < 4
    quads = [
        jnp.where(low, a, b) + pltpu.roll(jnp.where(low, b, a), 4, 0) for a, b in zip(tiles[:4], tiles[4:])
    ]
    low = index % 4 < 2
    pairs = [
        jnp.where(low, a + pltpu.roll(a, 6, 0), b + pltpu.roll(b, 2, 0)) for a, b in zip(quads[:2], quads[2:])
    ]
    a, b = pairs
    return jnp.where(index % 2 < 1, a + pltpu.roll(a, 7, 0), b + pltpu.roll(b, 1, 0))


def relay_kernel(position_ref, map_ref, slots_ref, grad_ref, gains_ref, out_ref, held_ref, normed_ref, sem):
    layers, rows, channels = normed_ref.shape
    slot_count = slots_ref.shape[0] // out_ref.shape[0]
    columns = [slice(at, at + lanes) for at in range(0, channels, lanes)]
    share = 1.0 / channels
    fetch = pltpu.make_async_copy(grad_ref.at[position_ref[0]], held_ref, sem)
    fetch.start()
    places, slot = [], 0
    for layer in range(layers):
        if layer:
            slot = jnp.where(map_ref[layer] == map_ref[layer - 1], slot + 1, 0)
        places.append(map_ref[layer] * slot_count + slot)

    def tiles(layer):
        return [slots_ref[places[layer], :, at].astype(jnp.float32) for at in columns]

    order = list(reversed(range(layers)))
    average = {layer: across(total(tiles(layer))) * share for layer in order}
    inverse = {}
    for layer in order:
        centered = [tile - average[layer] for tile in tiles(layer)]
        inverse[layer] = lax.rsqrt(across(total([tile * tile for tile in centered])) * share + epsilon)
    for layer in order:
        for at, tile in zip(columns, tiles(layer)):
            normed_ref[layer, :, at] = (tile - average[layer]) * inverse[layer]
    fetch.wait()
    gradient = [held_ref[:, at].astype(jnp.float32) for at in columns]
    blank = jnp.zeros((rows, lanes), jnp.float32)
    for layer in order:
        normed = [normed_ref[layer, :, at] for at in columns]
        along = [g * n for g, n in zip(gradient, normed)]
        gain = [gains_ref[layer:layer + 1, at] for at in columns]
        scaled = [g * c for g, c in zip(gradient, gain)]
        along_one = across(total(scaled)) * share * inverse[layer]
        along_normed = across(total([p * c for p, c in zip(along, gain)])) * share * inverse[layer]
        sums = along + gradient
        sums = sums + [blank] * (-len(sums) % 16)
        row = layers - 1 - layer
        for at in range(0, len(sums), 16):
            packed = jnp.concatenate([fold(sums[at:at + 8]), fold(sums[at + 8:at + 16])], axis=0)
            out_ref[row, at:at + 16] = packed.astype(out_ref.dtype)
        gradient = [
            ((g + inverse[layer] * u) - (along_one + along_normed * n)).astype(jnp.bfloat16).astype(jnp.float32)
            for g, u, n in zip(gradient, scaled, normed)
        ]


def relay(position, section_map, slots, grad, gains):
    layers, channels = gains.shape
    _, rows, _ = grad.shape
    packed_rows = -(-2 * channels // lanes // 16) * 16
    return pl.pallas_call(
        relay_kernel,
        grid_spec=pltpu.PrefetchScalarGridSpec(
            num_scalar_prefetch=2,
            grid=(),
            in_specs=[
                pl.BlockSpec(memory_space=pltpu.VMEM),
                pl.BlockSpec(memory_space=pl.ANY),
                pl.BlockSpec(memory_space=pltpu.VMEM),
            ],
            out_specs=pl.BlockSpec(memory_space=pltpu.VMEM),
            scratch_shapes=[
                pltpu.VMEM((rows, channels), grad.dtype),
                pltpu.VMEM((layers, rows, channels), jnp.float32),
                pltpu.SemaphoreType.DMA,
            ],
        ),
        out_shape=jax.ShapeDtypeStruct((layers, packed_rows, lanes), jnp.bfloat16),
        compiler_params=pltpu.CompilerParams(vmem_limit_bytes=24 * 1024 * 1024),
        cost_estimate=pl.CostEstimate(
            flops=30 * layers * rows * channels, bytes_accessed=4 * layers * rows * channels, transcendentals=0
        ),
    )(position, section_map, slots, grad, gains)


def summed(block, axis):
    received = lax.all_to_all(block, axis, 0, 0)
    return jnp.sum(received.astype(jnp.float32), axis=0)


def local(activations, grad_output, gains, layer_section):
    saved = activations[0, 0]
    slot_count, tokens, channels = saved.shape
    layers = gains.shape[0]
    sections = lax.axis_size("section")
    replicas = lax.axis_size("replica")
    position = jnp.full((1,), lax.axis_index("section"), jnp.int32)
    rows = tokens // sections
    blocks = deal(saved.reshape(slot_count, sections, rows, channels))
    received = lax.all_to_all(blocks, "section", 0, 0)
    slots = received.reshape(sections * slot_count, rows, channels)
    grad = grad_output[0].reshape(sections, rows, channels)
    partials = relay(position, layer_section[0], slots, grad, gains)
    mine = summed(partials, "section")
    pieces = mine.reshape(-1)[: 2 * channels].reshape(2, replicas, channels // replicas)
    owned = summed(jnp.transpose(pieces, (1, 0, 2)), "replica") / replicas
    return (owned[:1], owned[1:])


def solution(mesh):
    placed = (
        P("replica", "section", None, None, None),
        P("replica", None, None),
        P(),
        P("replica", None),
    )
    return jax.shard_map(
        local,
        mesh=mesh,
        in_specs=placed,
        out_specs=(P("section", "replica"), P("section", "replica")),
        check_vma=False,
    )
```
